32 devices in a mesh: ctx: 16 (over z, y, x), head: 2 (over core).
Axes of the slice: x: 2, y: 2, z: 4, core: 2. Of those that a mesh axis runs over, the one named last changes fastest.
Arguments:
- query_in: float32 [16384, 16, 128], P('ctx', 'head'), may hold values from -6 to 6
- key_in: float32 [16384, 16, 128], P('ctx', 'head'), may hold values from -6 to 6
- value_in: float32 [16384, 32, 128], P('ctx', 'head'), may hold values from -6 to 6
- gate_in: float32 [16384, 32, 128], P('ctx', 'head'), may hold values from -6 to 6
- log_gate: float32 [32, 16384], P('head', 'ctx'), may hold values from -1 to 0, as said below
- strength: float32 [32, 16384], P('head', 'ctx'), may hold values from 0.005 to 0.05
- query_conv: float32 [4, 16, 128], P(None, 'head'), may hold values from -3 to 3
- key_conv: float32 [4, 16, 128], P(None, 'head'), may hold values from -3 to 3
- value_conv: float32 [4, 32, 128], P(None, 'head'), may hold values from -3 to 3
- norm_gain: float32 [128], replicated, may hold values from 0.1 to 1.9
- out_weight: bfloat16 [4096, 2048], P('head'), may hold values from -0.09375 to 0.09375
Outputs:
- mixed: float32 [16384, 2048], P(('ctx', 'head'))
The draws below stay inside these ranges and needn't reach their ends.
Inputs may be any that keep to these rules, and one draw needn't show every extreme that they name: `log_gate`: the logarithm of head h's decay factor at a token.
All inputs are finite; a program needn't handle non-finite values.
Results may differ from the reference program's by a relative error of at most 0.015.
Values may be sent and summed in bfloat16 or wider, within the bound.
A program may use at most 192 MiB of HBM per device.

```python
import math
import jax
import jax.numpy as jnp
from jax import lax

D = 2048
PAYLOAD_GROUPS = 32
KHEADS = 16
DK = 128
DV = 128
CONV = 4
SPAN = 64
STREAM_LENGTH = 16384
N_HEAD = 2


def draw_log_gate(key, part):
    attention_group_seed, position_seed, location_seed, contiguous_seed = jax.random.split(jax.random.fold_in(key, 17), 4)
    spread = jax.random.uniform(attention_group_seed, (PAYLOAD_GROUPS, 1), jnp.float32, 0.0, 1.0)
    log_rate = math.log(1.0 / 40.0) * (1.0 - spread) + math.log(0.1 / STREAM_LENGTH) * spread
    unmasked_result = -jnp.exp(log_rate) * jax.random.uniform(position_seed, (PAYLOAD_GROUPS, STREAM_LENGTH), jnp.float32, 0.5, 1.5)
    places = jax.random.randint(location_seed, (PAYLOAD_GROUPS, 4), 0, STREAM_LENGTH)
    positions = jnp.arange(STREAM_LENGTH, dtype=jnp.int32)
    zeroed_elements = jnp.any(positions[None, None, :] == places[:, :, None], axis=1)
    contiguous_erasure = jnp.log(jax.random.uniform(contiguous_seed, (PAYLOAD_GROUPS, STREAM_LENGTH), jnp.float32, 0.5, 0.8))
    return jnp.where(zeroed_elements, unmasked_result + contiguous_erasure, unmasked_result)


def levels(key, shape, cuts, least, largest):
    level = 1.0
    for axis_at, blocks in cuts:
        steps = jax.random.uniform(jax.random.fold_in(jax.random.fold_in(key, 6), axis_at), (blocks,), jnp.float32, least / len(cuts), largest / len(cuts))
        level = level * jnp.repeat(jnp.exp(steps), shape[axis_at] // blocks).reshape((-1,) + (1,) * (len(shape) - 1 - axis_at))
    return level


def bell_draw(stream_key, shape, scale, most, shards=(), kind=jnp.bfloat16):
    values = jax.random.normal(stream_key, shape, jnp.float32) * scale
    if len(shards) > 0:
        values = levels(stream_key, shape, shards, -0.22, 0.18) * values
    return jnp.clip(values, min=-most, max=most).astype(kind)


def setup_inputs(seed: int = 0) -> dict:
    splits = jax.random.split(jax.random.key(seed), 12)
    query_in = bell_draw(splits[0], (STREAM_LENGTH, KHEADS, DK), 1.0, 6.0, ((0, 16), (1, 2)), jnp.float32)
    key_in = bell_draw(splits[1], (STREAM_LENGTH, KHEADS, DK), 1.0, 6.0, ((0, 16), (1, 2)), jnp.float32)
    value_in = bell_draw(splits[2], (STREAM_LENGTH, PAYLOAD_GROUPS, DV), 1.0, 6.0, ((0, 16), (1, 2)), jnp.float32)
    gate_in = bell_draw(splits[3], (STREAM_LENGTH, PAYLOAD_GROUPS, DV), 1.0, 6.0, ((0, 16), (1, 2)), jnp.float32)
    log_gate = draw_log_gate(jax.random.fold_in(splits[11], 71), 0)
    strength = jnp.clip(jnp.exp(math.log(0.05) - 2.3025851 * jax.random.uniform(splits[5], (PAYLOAD_GROUPS, STREAM_LENGTH), jnp.float32) ** levels(splits[5], (PAYLOAD_GROUPS, STREAM_LENGTH), ((0, 2), (1, 16)), -0.2, 0.2)), 0.005, 0.05)
    query_conv = bell_draw(splits[6], (CONV, KHEADS, DK), CONV ** -0.5, 3.0, ((1, 2),), jnp.float32)
    key_conv = bell_draw(splits[7], (CONV, KHEADS, DK), CONV ** -0.5, 3.0, ((1, 2),), jnp.float32)
    value_conv = bell_draw(splits[8], (CONV, PAYLOAD_GROUPS, DV), CONV ** -0.5, 3.0, ((1, 2),), jnp.float32)
    norm_gain = jnp.clip(1.0 + 0.18 * jax.random.normal(splits[9], (DV,), jnp.float32), 0.1, 1.9)
    out_weight = bell_draw(splits[10], (PAYLOAD_GROUPS * DV, D), (PAYLOAD_GROUPS * DV) ** -0.5, 0.09375, ((0, 2),))
    return dict(query_in=query_in, key_in=key_in, value_in=value_in, gate_in=gate_in, log_gate=log_gate, strength=strength, query_conv=query_conv, key_conv=key_conv, value_conv=value_conv, norm_gain=norm_gain, out_weight=out_weight)


exact_precision = lax.Precision.HIGHEST
norm_epsilon = 1e-06

def causal_mix(current, previous, kernel):
    kernel_width = kernel.shape[0]
    token_count = current.shape[0]
    padded = jnp.concatenate([previous, current], axis=0)
    summed = jnp.zeros(current.shape, jnp.float32)
    for offset in range(kernel_width):
        summed = summed + kernel[offset] * padded[offset:offset + token_count]
    return jax.nn.silu(summed)

def unit_rows(matrix):
    return matrix * lax.rsqrt(lax.optimization_barrier(jnp.sum(matrix * matrix, axis=-1, keepdims=True)) + norm_epsilon)

def to_blocks(matrix, block_size):
    token_count, head_count, width_count = matrix.shape
    return matrix.reshape(token_count // block_size, block_size, head_count, width_count).transpose(0, 2, 1, 3)

def gate_blocks(matrix, block_size):
    head_count, token_count = matrix.shape
    return matrix.reshape(head_count, token_count // block_size, block_size).transpose(1, 0, 2)

def prepare(query_in, key_in, value_in, query_prev, key_prev, value_prev, query_conv, key_conv, value_conv, block_size):
    group_ratio = value_in.shape[1] // query_in.shape[1]
    queries = unit_rows(causal_mix(query_in, query_prev, query_conv)) * query_in.shape[2] ** (-0.5)
    key_rows = unit_rows(causal_mix(key_in, key_prev, key_conv))
    values = causal_mix(value_in, value_prev, value_conv)
    queries = jnp.repeat(queries, group_ratio, axis=1)
    key_rows = jnp.repeat(key_rows, group_ratio, axis=1)
    return (to_blocks(queries, block_size), to_blocks(key_rows, block_size), to_blocks(values, block_size))

def unit_inverse(mixing):
    block_size = mixing.shape[-1]
    identity_map = jnp.eye(block_size, dtype=jnp.float32)
    powered = -mixing
    inverse = identity_map + powered
    reach = 2
    while reach < block_size:
        powered = jnp.einsum('nhij,nhjk->nhik', powered, powered, precision=exact_precision)
        inverse = jnp.einsum('nhij,nhjk->nhik', inverse, identity_map + powered, precision=exact_precision)
        reach = reach * 2
    return inverse

def span_setup(queries, key_rows, values, log_gate, strength):
    cumulative = jnp.cumsum(log_gate, axis=-1)
    block_size = cumulative.shape[-1]
    row_index = lax.broadcasted_iota(jnp.int32, (block_size, block_size), 0)
    col_index = lax.broadcasted_iota(jnp.int32, (block_size, block_size), 1)
    lower_mask = row_index >= col_index
    strict_mask = row_index > col_index
    differences = cumulative[..., :, None] - cumulative[..., None, :]
    decay_table = jnp.exp(jnp.where(lower_mask, differences, -jnp.inf))
    key_inner = jnp.einsum('nhcd,nhmd->nhcm', key_rows, key_rows, precision=exact_precision)
    mixing = jnp.where(strict_mask, strength[..., :, None] * key_inner * decay_table, 0.0)
    scores = jnp.where(lower_mask, jnp.einsum('nhcd,nhmd->nhcm', queries, key_rows, precision=exact_precision) * decay_table, 0.0)
    inverse = unit_inverse(mixing)
    fresh_values = jnp.einsum('nhcm,nhmw->nhcw', inverse, strength[..., None] * values, precision=exact_precision)
    solved_keys = jnp.einsum('nhcm,nhmd->nhcd', inverse, (strength * jnp.exp(cumulative))[..., None] * key_rows, precision=exact_precision)
    lifted = jnp.exp(cumulative)[..., None] * queries
    carried = jnp.exp(cumulative[..., -1:] - cumulative)[..., None] * key_rows
    ending = jnp.exp(cumulative[..., -1])
    return (fresh_values, solved_keys, scores, lifted, carried, ending)

def run_spans(start_state, setup, with_outputs):

    def advance(carry_state, per_span):
        fresh_block, solved_block, score_block, lifted_block, carried_block, ending_block = per_span
        update = fresh_block - jnp.einsum('hcd,hdw->hcw', solved_block, carry_state, precision=exact_precision)
        new_state = ending_block[:, None, None] * carry_state + jnp.einsum('hcd,hcw->hdw', carried_block, update, precision=exact_precision)
        if with_outputs:
            result = jnp.einsum('hcd,hdw->hcw', lifted_block, carry_state, precision=exact_precision)
            result = result + jnp.einsum('hcm,hmw->hcw', score_block, update, precision=exact_precision)
            return (new_state, result)
        return (new_state, None)
    return lax.scan(advance, start_state, setup)

def gated_norm(recurrent, gate_in, norm_gain):
    scaled = recurrent * lax.rsqrt(lax.optimization_barrier(jnp.mean(recurrent * recurrent, axis=-1, keepdims=True)) + norm_epsilon)
    return scaled * norm_gain * jax.nn.silu(gate_in)

def reference(query_in, key_in, value_in, gate_in, log_gate, strength, query_conv, key_conv, value_conv, norm_gain, out_weight):
    query_prev = jnp.zeros((CONV - 1, KHEADS, DK), jnp.float32)
    key_prev = jnp.zeros((CONV - 1, KHEADS, DK), jnp.float32)
    value_prev = jnp.zeros((CONV - 1, PAYLOAD_GROUPS, DV), jnp.float32)
    queries, key_rows, values = prepare(query_in, key_in, value_in, query_prev, key_prev, value_prev, query_conv, key_conv, value_conv, SPAN)
    setup = span_setup(queries, key_rows, values, gate_blocks(log_gate, SPAN), gate_blocks(strength, SPAN))
    start_state = jnp.zeros((PAYLOAD_GROUPS, DK, DV), jnp.float32)
    final_state, recurrent = run_spans(start_state, setup, True)
    recurrent = recurrent.transpose(0, 2, 1, 3).reshape(STREAM_LENGTH, PAYLOAD_GROUPS, DV)
    normed = gated_norm(recurrent, gate_in, norm_gain).astype(jnp.bfloat16).reshape(STREAM_LENGTH, PAYLOAD_GROUPS * DV)
    group_width = PAYLOAD_GROUPS // N_HEAD * DV
    mixed = jnp.zeros((STREAM_LENGTH, D), jnp.float32)
    for group_index in range(N_HEAD):
        first = group_index * group_width
        partial_value = jnp.dot(normed[:, first:first + group_width], out_weight[first:first + group_width], preferred_element_type=jnp.float32)
        rounded = lax.optimization_barrier(partial_value.astype(jnp.bfloat16))
        mixed = mixed + rounded.astype(jnp.float32)
    return mixed
```

```python
import jax
import jax.numpy as jnp
from jax import lax
from jax.sharding import PartitionSpec as P

SPAN = 64


exact_precision = lax.Precision.HIGHEST
norm_epsilon = 1e-06


def from_behind(value, axis, steps):
    count = lax.axis_size(axis)
    initial, last = (max(0, -steps), min(count, count - steps))
    return lax.ppermute(value, axis, [(source, source + steps) for source in range(initial, last)])


def causal_mix(current, previous, kernel):
    kernel_width = kernel.shape[0]
    token_count = current.shape[0]
    padded = jnp.concatenate([previous, current], axis=0)
    summed = jnp.zeros(current.shape, jnp.float32)
    for offset in range(kernel_width):
        summed = summed + kernel[offset] * padded[offset : offset + token_count]
    return jax.nn.silu(summed)


def unit_rows(matrix):
    return matrix * lax.rsqrt(jnp.sum(matrix * matrix, axis=-1, keepdims=True) + norm_epsilon)


def to_blocks(matrix, block_size):
    token_count, head_count, width_count = matrix.shape
    return matrix.reshape(token_count // block_size, block_size, head_count, width_count).transpose(
        0, 2, 1, 3
    )


def gate_blocks(matrix, block_size):
    head_count, token_count = matrix.shape
    return matrix.reshape(head_count, token_count // block_size, block_size).transpose(1, 0, 2)


def prepare(
    query_in,
    key_in,
    value_in,
    query_prev,
    key_prev,
    value_prev,
    query_conv,
    key_conv,
    value_conv,
    block_size,
):
    group_ratio = value_in.shape[1] // query_in.shape[1]
    queries = unit_rows(causal_mix(query_in, query_prev, query_conv)) * query_in.shape[2] ** (-0.5)
    key_rows = unit_rows(causal_mix(key_in, key_prev, key_conv))
    values = causal_mix(value_in, value_prev, value_conv)
    queries = jnp.repeat(queries, group_ratio, axis=1)
    key_rows = jnp.repeat(key_rows, group_ratio, axis=1)
    return (
        to_blocks(queries, block_size),
        to_blocks(key_rows, block_size),
        to_blocks(values, block_size),
    )


def unit_inverse(mixing):
    block_size = mixing.shape[-1]
    identity_map = jnp.eye(block_size, dtype=jnp.float32)
    powered = -mixing
    inverse = identity_map + powered
    reach = 2
    while reach < block_size:
        powered = jnp.einsum("nhij,nhjk->nhik", powered, powered, precision=exact_precision)
        inverse = jnp.einsum(
            "nhij,nhjk->nhik", inverse, identity_map + powered, precision=exact_precision
        )
        reach = reach * 2
    return inverse


def span_setup(queries, key_rows, values, log_gate, strength):
    block_size = log_gate.shape[-1]
    upper = jnp.triu(jnp.ones((block_size, block_size), jnp.float32))
    cumulative = jnp.einsum("nhm,mc->nhc", log_gate, upper, precision=exact_precision)
    row_index = lax.broadcasted_iota(jnp.int32, (block_size, block_size), 0)
    col_index = lax.broadcasted_iota(jnp.int32, (block_size, block_size), 1)
    lower_mask = row_index >= col_index
    strict_mask = row_index > col_index
    differences = cumulative[..., :, None] - cumulative[..., None, :]
    decay_table = jnp.exp(jnp.where(lower_mask, differences, -jnp.inf))
    key_inner = jnp.einsum("nhcd,nhmd->nhcm", key_rows, key_rows, precision=exact_precision)
    mixing = jnp.where(strict_mask, strength[..., :, None] * key_inner * decay_table, 0.0)
    scores = jnp.where(
        lower_mask,
        jnp.einsum("nhcd,nhmd->nhcm", queries, key_rows, precision=exact_precision) * decay_table,
        0.0,
    )
    inverse = unit_inverse(mixing)
    fresh_values = jnp.einsum(
        "nhcm,nhmw->nhcw", inverse, strength[..., None] * values, precision=exact_precision
    )
    solved_keys = jnp.einsum(
        "nhcm,nhmd->nhcd",
        inverse,
        (strength * jnp.exp(cumulative))[..., None] * key_rows,
        precision=exact_precision,
    )
    lifted = jnp.exp(cumulative)[..., None] * queries
    carried = jnp.exp(cumulative[..., -1:] - cumulative)[..., None] * key_rows
    ending = jnp.exp(cumulative[..., -1])
    return (fresh_values, solved_keys, scores, lifted, carried, ending)


def run_spans(start_state, setup):

    def advance(carry_state, per_span):
        fresh_block, solved_block, score_block, lifted_block, carried_block, ending_block = per_span
        update = fresh_block - jnp.einsum(
            "hcd,hdw->hcw", solved_block, carry_state, precision=exact_precision
        )
        new_state = ending_block[:, None, None] * carry_state + jnp.einsum(
            "hcd,hcw->hdw", carried_block, update, precision=exact_precision
        )
        result = jnp.einsum("hcd,hdw->hcw", lifted_block, carry_state, precision=exact_precision)
        result = result + jnp.einsum("hcm,hmw->hcw", score_block, update, precision=exact_precision)
        return (new_state, result)

    return lax.scan(advance, start_state, setup)


def gated_norm(recurrent, gate_in, norm_gain):
    scaled = recurrent * lax.rsqrt(
        jnp.mean(recurrent * recurrent, axis=-1, keepdims=True) + norm_epsilon
    )
    return scaled * norm_gain * jax.nn.silu(gate_in)


def batched(left, right):
    return jnp.einsum("hij,hjk->hik", left, right, precision=exact_precision)


def on_device(
    query_in,
    key_in,
    value_in,
    gate_in,
    log_gate,
    strength,
    query_conv,
    key_conv,
    value_conv,
    norm_gain,
    out_weight,
):
    rim_count = query_conv.shape[0] - 1
    query_prev, key_prev, value_prev = from_behind(
        (query_in[-rim_count:], key_in[-rim_count:], value_in[-rim_count:]), "ctx", 1
    )
    queries, key_rows, values = prepare(
        query_in,
        key_in,
        value_in,
        query_prev,
        key_prev,
        value_prev,
        query_conv,
        key_conv,
        value_conv,
        SPAN,
    )
    setup = span_setup(
        queries, key_rows, values, gate_blocks(log_gate, SPAN), gate_blocks(strength, SPAN)
    )
    fresh_values, solved_keys, scores, lifted, carried, ending = setup
    token_count = query_in.shape[0]
    head_dev = values.shape[1]
    key_width = key_rows.shape[3]
    value_width = values.shape[3]
    identity_map = jnp.broadcast_to(
        jnp.eye(key_width, dtype=jnp.float32), (head_dev, key_width, key_width)
    )
    empty_state = jnp.zeros((head_dev, key_width, value_width), jnp.float32)
    start_state = jnp.concatenate([identity_map, empty_state], axis=2)
    widened = jnp.concatenate([jnp.zeros(key_rows.shape, jnp.float32), fresh_values], axis=3)
    widened_setup = (widened, solved_keys, scores, lifted, carried, ending)
    final_state, widened_out = run_spans(start_state, widened_setup)
    transition = final_state[:, :, :key_width]
    offset = final_state[:, :, key_width:]
    chain_count = lax.axis_size("ctx") - 1

    def chain_turn(turn_index, chain_carry):
        received = from_behind(chain_carry[1].astype(jnp.bfloat16), "ctx", 1).astype(jnp.float32)
        return (received, batched(transition, received) + offset)

    entering = lax.fori_loop(0, chain_count, chain_turn, (empty_state, offset))[0]
    recurrent = widened_out[..., key_width:] + jnp.einsum(
        "nhcd,hdw->nhcw", widened_out[..., :key_width], entering, precision=exact_precision
    )
    recurrent = recurrent.transpose(0, 2, 1, 3).reshape(token_count, head_dev, value_width)
    normed = (
        gated_norm(recurrent, gate_in, norm_gain)
        .astype(jnp.bfloat16)
        .reshape(token_count, head_dev * value_width)
    )
    return lax.psum_scatter(
        jnp.dot(normed, out_weight, preferred_element_type=jnp.float32).astype(jnp.bfloat16),
        "head",
        scatter_dimension=0,
        tiled=True,
    ).astype(jnp.float32)


def solution(mesh):
    in_specs = (
        P("ctx", "head", None),
        P("ctx", "head", None),
        P("ctx", "head", None),
        P("ctx", "head", None),
        P("head", "ctx"),
        P("head", "ctx"),
        P(None, "head", None),
        P(None, "head", None),
        P(None, "head", None),
        P(),
        P("head", None),
    )
    out_specs = P(("ctx", "head"), None)
    return jax.shard_map(
        on_device, mesh=mesh, in_specs=in_specs, out_specs=out_specs, check_vma=False
    )
```

```python
import functools

import jax
import jax.numpy as jnp
from jax import lax
from jax.experimental import pallas as pl
from jax.experimental.pallas import tpu as pltpu
from jax.sharding import PartitionSpec as P

norm_epsilon = 1e-06
CHUNK = 128
BASE = 32
RIM = 8
VMEM_LIMIT = 56 * 2**20


def mm(left, right):
    return jnp.dot(
        left.astype(jnp.bfloat16), right.astype(jnp.bfloat16), preferred_element_type=jnp.float32
    )


def silu(value):
    return value / (1.0 + jnp.exp(-value))


def from_behind(value, axis, steps):
    count = lax.axis_size(axis)
    return lax.ppermute(value, axis, [(s, s + steps) for s in range(max(0, count - steps))])


def conv_head(x_ref, rim_ref, w_ref, head, heads, chunk, taps):
    current = x_ref[pl.ds(head, chunk, stride=heads), :]
    padded = jnp.concatenate([rim_ref[pl.ds(head, RIM, stride=heads), :], current], axis=0)
    total = w_ref[(taps - 1) * heads + head : (taps - 1) * heads + head + 1, :] * current
    for back in range(1, taps):
        row = (taps - 1 - back) * heads + head
        total = total + w_ref[row : row + 1, :] * pltpu.roll(padded, back, 0)[RIM:]
    return silu(total)


def unit_rows(matrix, scale=1.0):
    total = jnp.sum(matrix * matrix, axis=-1, keepdims=True)
    return matrix * (lax.rsqrt(total + norm_epsilon) * scale)


def chunk_kernel(
    meta,
    q_ref,
    k_ref,
    v_ref,
    q_rim,
    k_rim,
    v_rim,
    q_w,
    k_w,
    v_w,
    crow_ref,
    ccol_ref,
    bcol_ref,
    out_ref,
    fin_ref,
    state,
    q_old,
    k_old,
    v_old,
):
    chunk, kheads, vheads, kfirst, kgroup, taps = meta
    ratio = vheads // kheads
    width = q_ref.shape[1]
    step = pl.program_id(0)

    @pl.when(step == 0)
    def _():
        q_old[...] = q_rim[...]
        k_old[...] = k_rim[...]
        v_old[...] = v_rim[...]
        row = lax.broadcasted_iota(jnp.int32, (width, 2 * width), 0)
        col = lax.broadcasted_iota(jnp.int32, (width, 2 * width), 1)
        start = jnp.where(row == col, 1.0, 0.0)
        for v in range(kgroup * ratio):
            state[v] = start

    row = lax.broadcasted_iota(jnp.int32, (chunk, chunk), 0)
    col = lax.broadcasted_iota(jnp.int32, (chunk, chunk), 1)
    lower = row >= col
    strict = row > col
    eye = jnp.where(row == col, 1.0, 0.0)

    def same(size):
        return (row // size) == (col // size)

    count = kgroup * ratio
    keys, keys_t, lifted, scores, mixing, rhs = [], [], [], [], [], []
    for i in range(kgroup):
        q = unit_rows(conv_head(q_ref, q_old, q_w, kfirst + i, kheads, chunk, taps), width**-0.5)
        k = unit_rows(conv_head(k_ref, k_old, k_w, kfirst + i, kheads, chunk, taps))
        k_t = k.T.astype(jnp.bfloat16)
        inner = mm(k, k_t)
        cross = mm(q, k_t)
        for r in range(ratio):
            v = i * ratio + r
            values = conv_head(v_ref, v_old, v_w, kfirst * ratio + v, vheads, chunk, taps)
            cc = ccol_ref[:, v : v + 1]
            b = bcol_ref[:, v : v + 1]
            decay = jnp.exp(jnp.minimum(cc - crow_ref[v : v + 1, :], 0.0))
            lift = jnp.exp(cc)
            mixing.append(jnp.where(strict, -(b * inner * decay), 0.0))
            scores.append(jnp.where(lower, cross * decay, 0.0).astype(jnp.bfloat16))
            lifted.append((lift * q).astype(jnp.bfloat16))
            rhs.append(
                jnp.concatenate([b * values, (b * lift) * k], axis=1).astype(jnp.bfloat16)
            )
            keys_t.append(k_t)

    base = min(BASE, chunk)
    near = same(base)
    power = [jnp.where(near, m, 0.0).astype(jnp.bfloat16) for m in mixing]
    inverse = [eye + p.astype(jnp.float32) for p in power]
    power = [mm(p, p).astype(jnp.bfloat16) for p in power]
    reach = 2
    while reach < base:
        if reach * 2 < base:
            both = [
                mm(jnp.concatenate([t.astype(jnp.bfloat16), p], axis=0), p)
                for t, p in zip(inverse, power)
            ]
            inverse = [t + x[:chunk] for t, x in zip(inverse, both)]
            power = [x[chunk:].astype(jnp.bfloat16) for x in both]
        else:
            inverse = [t + mm(t, p) for t, p in zip(inverse, power)]
        reach *= 2
    size = base
    while size < chunk:
        far = same(2 * size) & jnp.logical_not(same(size))
        halves = [t.astype(jnp.bfloat16) for t in inverse]
        links = [mm(jnp.where(far, m, 0.0), t) for m, t in zip(mixing, halves)]
        inverse = [t + mm(h, x) for t, h, x in zip(inverse, halves, links)]
        size *= 2

    solved = [mm(t, r) for t, r in zip(inverse, rhs)]
    states = [state[v] for v in range(count)]
    narrow = [s.astype(jnp.bfloat16) for s in states]
    taken = [mm(x[:, width:], s) for x, s in zip(solved, narrow)]
    update = [
        jnp.concatenate([-w[:, :width], x[:, :width] - w[:, width:]], axis=1)
        for w, x in zip(taken, solved)
    ]
    for v in range(count):
        left = jnp.concatenate([lifted[v], scores[v]], axis=1)
        right = jnp.concatenate([narrow[v], update[v].astype(jnp.bfloat16)], axis=0)
        out_ref[v] = mm(left, right).astype(out_ref.dtype)
        last = crow_ref[v : v + 1, chunk - 1 : chunk]
        fade = jnp.exp(last - ccol_ref[:, v : v + 1])
        state[v] = jnp.exp(last) * states[v] + mm(keys_t[v], fade * update[v])

    for old, ref, heads in ((q_old, q_ref, kheads), (k_old, k_ref, kheads), (v_old, v_ref, vheads)):
        old[...] = ref[(chunk - RIM) * heads : chunk * heads, :]

    @pl.when(step == pl.num_programs(0) - 1)
    def _():
        fin_ref[...] = state[...]


def chunk_call(meta, tokens, width, arrays):
    chunk, kheads, vheads, kfirst, kgroup, taps = meta
    count = kgroup * (vheads // kheads)
    group = kfirst // kgroup

    def whole(rows):
        return pl.BlockSpec((rows, width), lambda c: (0, 0))

    def part(rows):
        return pl.BlockSpec((rows, width), lambda c: (c, 0))

    flops = 2 * tokens * count * width * width * 20
    return pl.pallas_call(
        functools.partial(chunk_kernel, meta),
        grid=(tokens // chunk,),
        in_specs=[
            part(chunk * kheads),
            part(chunk * kheads),
            part(chunk * vheads),
            whole(RIM * kheads),
            whole(RIM * kheads),
            whole(RIM * vheads),
            whole(taps * kheads),
            whole(taps * kheads),
            whole(taps * vheads),
            pl.BlockSpec((count, chunk), lambda c: (group, c)),
            pl.BlockSpec((chunk, count), lambda c: (c, 0)),
            pl.BlockSpec((chunk, count), lambda c: (c, 0)),
        ],
        out_specs=[
            pl.BlockSpec((count, chunk, 2 * width), lambda c: (0, c, 0)),
            pl.BlockSpec((count, width, 2 * width), lambda c: (0, 0, 0)),
        ],
        out_shape=[
            jax.ShapeDtypeStruct((count, tokens, 2 * width), jnp.bfloat16),
            jax.ShapeDtypeStruct((count, width, 2 * width), jnp.float32),
        ],
        scratch_shapes=[
            pltpu.VMEM((count, width, 2 * width), jnp.float32),
            pltpu.VMEM((RIM * kheads, width), jnp.float32),
            pltpu.VMEM((RIM * kheads, width), jnp.float32),
            pltpu.VMEM((RIM * vheads, width), jnp.float32),
        ],
        compiler_params=pltpu.CompilerParams(
            dimension_semantics=("arbitrary",), vmem_limit_bytes=VMEM_LIMIT
        ),
        cost_estimate=pl.CostEstimate(
            flops=flops, bytes_accessed=24 * 2**20, transcendentals=tokens * count * width * 4
        ),
    )(*arrays)


def enter_state(final):
    width = final.shape[1]

    def compose(later, earlier):
        return jnp.einsum(
            "hij,hjk->hik",
            later[:, :, :width].astype(jnp.bfloat16),
            earlier,
            preferred_element_type=jnp.float32,
        )

    count = lax.axis_size("ctx")
    empty = jnp.zeros((final.shape[0], width, width), jnp.float32)
    pair, reach = final, 1
    while 2 * reach < count:
        earlier = from_behind(pair.astype(jnp.bfloat16), "ctx", reach)
        pair = compose(pair, earlier) + jnp.concatenate([empty, pair[:, :, width:]], axis=2)
        reach *= 2
    sent = pair.astype(jnp.bfloat16)
    near = from_behind(sent, "ctx", 1)
    far = from_behind(sent[:, :, width:], "ctx", reach + 1)
    return (compose(near, far) + near[:, :, width:].astype(jnp.float32)).astype(jnp.bfloat16)


def mix_kernel(groups, rows, vheads, first_ref, *refs):
    outs, enters = refs[:groups], refs[groups : 2 * groups]
    gate_ref, gain_ref, weight_ref, part_ref, normed = refs[2 * groups :]
    width = gain_ref.shape[1]
    count = vheads // groups
    for g in range(groups):
        for v in range(count):
            head = g * count + v
            own = outs[g][v]
            recurrent = own[:, width:].astype(jnp.float32) + mm(own[:, :width], enters[g][v])
            mean = jnp.sum(recurrent * recurrent, axis=-1, keepdims=True) * (1.0 / width)
            gate = gate_ref[pl.ds(head, rows, stride=vheads), :]
            scaled = recurrent * lax.rsqrt(mean + norm_epsilon) * gain_ref[...] * silu(gate)
            normed[:, head * width : (head + 1) * width] = scaled.astype(jnp.bfloat16)
    depth, columns = weight_ref.shape
    piece = min(512, columns)
    for c in range(0, columns, piece):
        part_ref[:, c : c + piece] = jnp.dot(
            normed[...], weight_ref[:, c : c + piece], preferred_element_type=jnp.float32
        ).astype(jnp.bfloat16)


def mix_call(first, tokens, outs, enters, gate, gain, weight):
    groups = len(outs)
    count, all_tokens, double = outs[0].shape
    width = double // 2
    vheads = gate.shape[0] // all_tokens
    rows = min(256, tokens)
    depth, columns = weight.shape
    spec = pltpu.PrefetchScalarGridSpec(
        num_scalar_prefetch=1,
        grid=(tokens // rows,),
        in_specs=[pl.BlockSpec((count, rows, double), lambda t, s: (0, s[0] + t, 0))] * groups
        + [pl.BlockSpec((count, width, width), lambda t, s: (0, 0, 0))] * groups
        + [
            pl.BlockSpec((rows * vheads, width), lambda t, s: (s[0] + t, 0)),
            pl.BlockSpec((1, width), lambda t, s: (0, 0)),
            pl.BlockSpec((depth, columns), lambda t, s: (0, 0)),
        ],
        out_specs=pl.BlockSpec((rows, columns), lambda t, s: (t, 0)),
        scratch_shapes=[pltpu.VMEM((rows, depth), jnp.bfloat16)],
    )
    return pl.pallas_call(
        functools.partial(mix_kernel, groups, rows, vheads),
        grid_spec=spec,
        out_shape=jax.ShapeDtypeStruct((tokens, columns), jnp.bfloat16),
        compiler_params=pltpu.CompilerParams(
            dimension_semantics=("arbitrary",), vmem_limit_bytes=VMEM_LIMIT
        ),
        cost_estimate=pl.CostEstimate(
            flops=2 * tokens * depth * columns,
            bytes_accessed=2 * depth * columns + 16 * tokens * depth,
            transcendentals=tokens * depth,
        ),
    )((first // rows).astype(jnp.int32).reshape(1), *outs, *enters, gate, gain, weight)


def on_device(
    query_in,
    key_in,
    value_in,
    gate_in,
    log_gate,
    strength,
    query_conv,
    key_conv,
    value_conv,
    norm_gain,
    out_weight,
):
    tokens, kheads, width = query_in.shape
    vheads = value_in.shape[1]
    taps = query_conv.shape[0]
    ratio = vheads // kheads
    chunk = min(CHUNK, tokens)
    rim = taps - 1

    def flat(array):
        return array.reshape(-1, width)

    rims = from_behind(
        jnp.concatenate([a[-rim:] for a in (query_in, key_in, value_in)], axis=1), "ctx", 1
    )
    rims = jnp.pad(rims, ((RIM - rim, 0), (0, 0), (0, 0)))
    q_rim, k_rim, v_rim = (
        flat(rims[:, a:b])
        for a, b in ((0, kheads), (kheads, 2 * kheads), (2 * kheads, 2 * kheads + vheads))
    )
    upper = jnp.triu(jnp.ones((chunk, chunk), jnp.float32))
    summed = jnp.einsum(
        "hnm,mc->hnc",
        log_gate.reshape(vheads, tokens // chunk, chunk),
        upper,
        precision=lax.Precision.HIGHEST,
    ).reshape(vheads, tokens)

    kgroup = min(4, kheads)
    outs, enters = [], []
    for kfirst in range(0, kheads, kgroup):
        picked = slice(kfirst * ratio, (kfirst + kgroup) * ratio)
        out, final = chunk_call(
            (chunk, kheads, vheads, kfirst, kgroup, taps),
            tokens,
            width,
            (
                flat(query_in),
                flat(key_in),
                flat(value_in),
                q_rim,
                k_rim,
                v_rim,
                flat(query_conv),
                flat(key_conv),
                flat(value_conv),
                summed,
                summed[picked].T,
                strength[picked].T,
            ),
        )
        outs.append(out)
        enters.append(enter_state(final))

    shares = lax.axis_size("head")
    gate = flat(gate_in)
    gain = norm_gain.reshape(1, width)
    mix = functools.partial(
        mix_call, outs=outs, enters=enters, gate=gate, gain=gain, weight=out_weight
    )
    if shares != 2:
        partial = mix(jnp.int32(0), tokens)
        return lax.psum_scatter(partial, "head", scatter_dimension=0, tiled=True).astype(
            jnp.float32
        )
    me = lax.axis_index("head")
    half = tokens // 2
    other = mix((1 - me) * half, half)
    arrived = lax.ppermute(other, "head", [(0, 1), (1, 0)])
    own = mix(me * half, half)
    return own.astype(jnp.float32) + arrived.astype(jnp.float32)


def solution(mesh):
    in_specs = (
        P("ctx", "head", None),
        P("ctx", "head", None),
        P("ctx", "head", None),
        P("ctx", "head", None),
        P("head", "ctx"),
        P("head", "ctx"),
        P(None, "head", None),
        P(None, "head", None),
        P(None, "head", None),
        P(),
        P("head", None),
    )
    out_specs = P(("ctx", "head"), None)
    return jax.shard_map(
        on_device, mesh=mesh, in_specs=in_specs, out_specs=out_specs, check_vma=False
    )
```

```python
import functools

import jax
import jax.numpy as jnp
from jax import lax
from jax.experimental import pallas as pl
from jax.experimental.pallas import tpu as pltpu
from jax.sharding import PartitionSpec as P

norm_epsilon = 1e-06
CHUNK = 128
BASE = 32
RIM = 8
VMEM_LIMIT = 56 * 2**20


def mm(left, right):
    return jnp.dot(
        left.astype(jnp.bfloat16), right.astype(jnp.bfloat16), preferred_element_type=jnp.float32
    )


def silu(value):
    return value / (1.0 + jnp.exp(-value))


def from_behind(value, axis, steps):
    count = lax.axis_size(axis)
    return lax.ppermute(value, axis, [(s, s + steps) for s in range(max(0, count - steps))])


def conv_head(x_ref, rim_ref, w_ref, head, heads, chunk, taps):
    current = x_ref[pl.ds(head, chunk, stride=heads), :]
    padded = jnp.concatenate([rim_ref[pl.ds(head, RIM, stride=heads), :], current], axis=0)
    total = w_ref[(taps - 1) * heads + head : (taps - 1) * heads + head + 1, :] * current
    for back in range(1, taps):
        row = (taps - 1 - back) * heads + head
        total = total + w_ref[row : row + 1, :] * pltpu.roll(padded, back, 0)[RIM:]
    return silu(total)


def unit_rows(matrix, scale=1.0):
    total = jnp.sum(matrix * matrix, axis=-1, keepdims=True)
    return matrix * (lax.rsqrt(total + norm_epsilon) * scale)


def chunk_kernel(
    meta,
    q_ref,
    k_ref,
    v_ref,
    q_rim,
    k_rim,
    v_rim,
    q_w,
    k_w,
    v_w,
    crow_ref,
    brow_ref,
    out_ref,
    fin_ref,
    state,
    q_old,
    k_old,
    v_old,
):
    chunk, kheads, vheads, kfirst, kgroup, taps = meta
    ratio = vheads // kheads
    width = q_ref.shape[1]
    step = pl.program_id(0)

    @pl.when(step == 0)
    def _():
        q_old[...] = q_rim[...]
        k_old[...] = k_rim[...]
        v_old[...] = v_rim[...]
        row = lax.broadcasted_iota(jnp.int32, (width, 2 * width), 0)
        col = lax.broadcasted_iota(jnp.int32, (width, 2 * width), 1)
        start = jnp.where(row == col, 1.0, 0.0)
        for v in range(kgroup * ratio):
            state[v] = start

    row = lax.broadcasted_iota(jnp.int32, (chunk, chunk), 0)
    col = lax.broadcasted_iota(jnp.int32, (chunk, chunk), 1)
    lower = row >= col
    strict = row > col
    eye = jnp.where(row == col, 1.0, 0.0)

    def same(size):
        return (row // size) == (col // size)

    count = kgroup * ratio
    ccol = crow_ref[...].T
    bcol = brow_ref[...].T
    keys_t, lifted, scores, mixing, rhs = [], [], [], [], []
    for i in range(kgroup):
        q = unit_rows(conv_head(q_ref, q_old, q_w, kfirst + i, kheads, chunk, taps), width**-0.5)
        k = unit_rows(conv_head(k_ref, k_old, k_w, kfirst + i, kheads, chunk, taps))
        k_t = k.T.astype(jnp.bfloat16)
        inner = mm(k, k_t)
        cross = mm(q, k_t)
        for r in range(ratio):
            v = i * ratio + r
            values = conv_head(v_ref, v_old, v_w, kfirst * ratio + v, vheads, chunk, taps)
            cc = ccol[:, v : v + 1]
            b = bcol[:, v : v + 1]
            decay = jnp.exp(jnp.minimum(cc - crow_ref[v : v + 1, :], 0.0))
            lift = jnp.exp(cc)
            mixing.append(jnp.where(strict, -(b * inner * decay), 0.0))
            scores.append(jnp.where(lower, cross * decay, 0.0).astype(jnp.bfloat16))
            lifted.append((lift * q).astype(jnp.bfloat16))
            rhs.append(
                jnp.concatenate([b * values, (b * lift) * k], axis=1).astype(jnp.bfloat16)
            )
            keys_t.append(k_t)

    base = min(BASE, chunk)
    near = same(base)
    power = [jnp.where(near, m, 0.0).astype(jnp.bfloat16) for m in mixing]
    inverse = [eye + p.astype(jnp.float32) for p in power]
    power = [mm(p, p).astype(jnp.bfloat16) for p in power]
    reach = 2
    while reach < base:
        if reach * 2 < base:
            both = [
                mm(jnp.concatenate([t.astype(jnp.bfloat16), p], axis=0), p)
                for t, p in zip(inverse, power)
            ]
            inverse = [t + x[:chunk] for t, x in zip(inverse, both)]
            power = [x[chunk:].astype(jnp.bfloat16) for x in both]
        else:
            inverse = [t + mm(t, p) for t, p in zip(inverse, power)]
        reach *= 2
    size = base
    while size < chunk:
        far = same(2 * size) & jnp.logical_not(same(size))
        halves = [t.astype(jnp.bfloat16) for t in inverse]
        links = [mm(jnp.where(far, m, 0.0), t) for m, t in zip(mixing, halves)]
        inverse = [t + mm(h, x) for t, h, x in zip(inverse, halves, links)]
        size *= 2

    solved = [mm(t, r) for t, r in zip(inverse, rhs)]
    states = [state[v] for v in range(count)]
    narrow = [s.astype(jnp.bfloat16) for s in states]
    taken = [mm(x[:, width:], s) for x, s in zip(solved, narrow)]
    update = [
        jnp.concatenate([-w[:, :width], x[:, :width] - w[:, width:]], axis=1)
        for w, x in zip(taken, solved)
    ]
    for v in range(count):
        left = jnp.concatenate([lifted[v], scores[v]], axis=1)
        right = jnp.concatenate([narrow[v], update[v].astype(jnp.bfloat16)], axis=0)
        out_ref[v] = mm(left, right).astype(out_ref.dtype)
        last = crow_ref[v : v + 1, chunk - 1 : chunk]
        fade = jnp.exp(last - ccol[:, v : v + 1])
        state[v] = jnp.exp(last) * states[v] + mm(keys_t[v], fade * update[v])

    for old, ref, heads in ((q_old, q_ref, kheads), (k_old, k_ref, kheads), (v_old, v_ref, vheads)):
        old[...] = ref[(chunk - RIM) * heads : chunk * heads, :]

    @pl.when(step == pl.num_programs(0) - 1)
    def _():
        fin_ref[...] = state[...]


def chunk_call(meta, tokens, width, arrays):
    chunk, kheads, vheads, kfirst, kgroup, taps = meta
    count = kgroup * (vheads // kheads)
    group = kfirst // kgroup

    def whole(rows):
        return pl.BlockSpec((rows, width), lambda c: (0, 0))

    def part(rows):
        return pl.BlockSpec((rows, width), lambda c: (c, 0))

    flops = 2 * tokens * count * width * width * 20
    return pl.pallas_call(
        functools.partial(chunk_kernel, meta),
        grid=(tokens // chunk,),
        in_specs=[
            part(chunk * kheads),
            part(chunk * kheads),
            part(chunk * vheads),
            whole(RIM * kheads),
            whole(RIM * kheads),
            whole(RIM * vheads),
            whole(taps * kheads),
            whole(taps * kheads),
            whole(taps * vheads),
            pl.BlockSpec((count, chunk), lambda c: (group, c)),
            pl.BlockSpec((count, chunk), lambda c: (group, c)),
        ],
        out_specs=[
            pl.BlockSpec((count, chunk, 2 * width), lambda c: (0, c, 0)),
            pl.BlockSpec((count, width, 2 * width), lambda c: (0, 0, 0)),
        ],
        out_shape=[
            jax.ShapeDtypeStruct((count, tokens, 2 * width), jnp.bfloat16),
            jax.ShapeDtypeStruct((count, width, 2 * width), jnp.float32),
        ],
        scratch_shapes=[
            pltpu.VMEM((count, width, 2 * width), jnp.float32),
            pltpu.VMEM((RIM * kheads, width), jnp.float32),
            pltpu.VMEM((RIM * kheads, width), jnp.float32),
            pltpu.VMEM((RIM * vheads, width), jnp.float32),
        ],
        compiler_params=pltpu.CompilerParams(
            dimension_semantics=("arbitrary",), vmem_limit_bytes=VMEM_LIMIT
        ),
        cost_estimate=pl.CostEstimate(
            flops=flops, bytes_accessed=24 * 2**20, transcendentals=tokens * count * width * 4
        ),
    )(*arrays)


def chain_kernel(groups, *refs):
    finals, enter_ref = refs[:groups], refs[groups]
    arrived, leaving, send_sem, recv_sem = refs[groups + 1 :]
    n = lax.axis_size("ctx")
    me = lax.axis_index("ctx")
    right, left = lax.rem(me + 1, n), lax.rem(me + n - 1, n)
    count, width = finals[0].shape[0], finals[0].shape[1]

    barrier = pltpu.get_barrier_semaphore()
    for neighbour in (left, right):
        pl.semaphore_signal(
            barrier, inc=1, device_id={"ctx": neighbour}, device_id_type=pl.DeviceIdType.MESH
        )
    pl.semaphore_wait(barrier, 2)

    def hop(head):
        return pltpu.make_async_remote_copy(
            src_ref=leaving.at[head],
            dst_ref=arrived.at[head],
            send_sem=send_sem.at[head],
            recv_sem=recv_sem.at[head],
            device_id={"ctx": right},
            device_id_type=pl.DeviceIdType.MESH,
        )

    for g in range(groups):
        final = finals[g]

        def turn(v, carry, final=final, g=g):
            head = g * count + v

            @pl.when(me == 0)
            def _():
                enter_ref[head] = jnp.zeros((width, width), jnp.bfloat16)
                leaving[head] = final[v, :, width:].astype(jnp.bfloat16)

            @pl.when(me > 0)
            def _():
                hop(head).wait_recv()
                received = arrived[head]
                enter_ref[head] = received
                leaving[head] = (
                    mm(final[v, :, :width], received) + final[v, :, width:]
                ).astype(jnp.bfloat16)

            @pl.when(me < n - 1)
            def _():
                hop(head).start()

            return carry

        lax.fori_loop(0, count, turn, 0)

    @pl.when(me < n - 1)
    def _():
        def settle(head, carry):
            hop(head).wait_send()
            return carry

        lax.fori_loop(0, groups * count, settle, 0)


def enter_states(finals):
    groups = len(finals)
    count, width, _ = finals[0].shape
    heads = groups * count
    return pl.pallas_call(
        functools.partial(chain_kernel, groups),
        out_shape=jax.ShapeDtypeStruct((heads, width, width), jnp.bfloat16),
        in_specs=[pl.BlockSpec(memory_space=pltpu.VMEM)] * groups,
        out_specs=pl.BlockSpec(memory_space=pltpu.VMEM),
        scratch_shapes=[
            pltpu.VMEM((heads, width, width), jnp.bfloat16),
            pltpu.VMEM((heads, width, width), jnp.bfloat16),
            pltpu.SemaphoreType.DMA((heads,)),
            pltpu.SemaphoreType.DMA((heads,)),
        ],
        compiler_params=pltpu.CompilerParams(
            collective_id=0, has_side_effects=True, vmem_limit_bytes=VMEM_LIMIT
        ),
        cost_estimate=pl.CostEstimate(
            flops=2 * heads * width**3, bytes_accessed=12 * heads * width**2, transcendentals=0
        ),
    )(*finals)


def mix_kernel(groups, rows, vheads, first_ref, *refs):
    outs = refs[:groups]
    enter_ref, gate_ref, gain_ref, weight_ref, part_ref, normed = refs[groups:]
    width = gain_ref.shape[1]
    count = vheads // groups
    for g in range(groups):
        for v in range(count):
            head = g * count + v
            own = outs[g][v]
            recurrent = own[:, width:].astype(jnp.float32) + mm(own[:, :width], enter_ref[head])
            mean = jnp.sum(recurrent * recurrent, axis=-1, keepdims=True) * (1.0 / width)
            gate = gate_ref[pl.ds(head, rows, stride=vheads), :]
            scaled = recurrent * lax.rsqrt(mean + norm_epsilon) * gain_ref[...] * silu(gate)
            normed[:, head * width : (head + 1) * width] = scaled.astype(jnp.bfloat16)
    depth, columns = weight_ref.shape
    piece = min(512, columns)
    for c in range(0, columns, piece):
        part_ref[:, c : c + piece] = jnp.dot(
            normed[...], weight_ref[:, c : c + piece], preferred_element_type=jnp.float32
        ).astype(jnp.bfloat16)


def mix_call(first, tokens, outs, enters, gate, gain, weight):
    groups = len(outs)
    count, all_tokens, double = outs[0].shape
    width = double // 2
    vheads = gate.shape[0] // all_tokens
    rows = min(256, tokens)
    depth, columns = weight.shape
    spec = pltpu.PrefetchScalarGridSpec(
        num_scalar_prefetch=1,
        grid=(tokens // rows,),
        in_specs=[pl.BlockSpec((count, rows, double), lambda t, s: (0, s[0] + t, 0))] * groups
        + [
            pl.BlockSpec((vheads, width, width), lambda t, s: (0, 0, 0)),
            pl.BlockSpec((rows * vheads, width), lambda t, s: (s[0] + t, 0)),
            pl.BlockSpec((1, width), lambda t, s: (0, 0)),
            pl.BlockSpec((depth, columns), lambda t, s: (0, 0)),
        ],
        out_specs=pl.BlockSpec((rows, columns), lambda t, s: (t, 0)),
        scratch_shapes=[pltpu.VMEM((rows, depth), jnp.bfloat16)],
    )
    return pl.pallas_call(
        functools.partial(mix_kernel, groups, rows, vheads),
        grid_spec=spec,
        out_shape=jax.ShapeDtypeStruct((tokens, columns), jnp.bfloat16),
        compiler_params=pltpu.CompilerParams(
            dimension_semantics=("arbitrary",), vmem_limit_bytes=VMEM_LIMIT
        ),
        cost_estimate=pl.CostEstimate(
            flops=2 * tokens * depth * columns,
            bytes_accessed=2 * depth * columns + 16 * tokens * depth,
            transcendentals=tokens * depth,
        ),
    )((first // rows).astype(jnp.int32).reshape(1), *outs, enters, gate, gain, weight)


def on_device(
    query_in,
    key_in,
    value_in,
    gate_in,
    log_gate,
    strength,
    query_conv,
    key_conv,
    value_conv,
    norm_gain,
    out_weight,
):
    tokens, kheads, width = query_in.shape
    vheads = value_in.shape[1]
    taps = query_conv.shape[0]
    ratio = vheads // kheads
    chunk = min(CHUNK, tokens)
    rim = taps - 1

    def flat(array):
        return array.reshape(-1, width)

    rims = from_behind(
        jnp.concatenate([a[-rim:] for a in (query_in, key_in, value_in)], axis=1), "ctx", 1
    )
    rims = jnp.pad(rims, ((RIM - rim, 0), (0, 0), (0, 0)))
    q_rim, k_rim, v_rim = (
        flat(rims[:, a:b])
        for a, b in ((0, kheads), (kheads, 2 * kheads), (2 * kheads, 2 * kheads + vheads))
    )
    upper = jnp.triu(jnp.ones((chunk, chunk), jnp.float32))
    summed = jnp.einsum(
        "hnm,mc->hnc",
        log_gate.reshape(vheads, tokens // chunk, chunk),
        upper,
        precision=lax.Precision.HIGHEST,
    ).reshape(vheads, tokens)

    kgroup = min(4, kheads)
    outs, finals = [], []
    for kfirst in range(0, kheads, kgroup):
        out, final = chunk_call(
            (chunk, kheads, vheads, kfirst, kgroup, taps),
            tokens,
            width,
            (
                flat(query_in),
                flat(key_in),
                flat(value_in),
                q_rim,
                k_rim,
                v_rim,
                flat(query_conv),
                flat(key_conv),
                flat(value_conv),
                summed,
                strength,
            ),
        )
        outs.append(out)
        finals.append(final)
    enters = enter_states(finals)

    shares = lax.axis_size("head")
    gate = flat(gate_in)
    gain = norm_gain.reshape(1, width)
    mix = functools.partial(
        mix_call, outs=outs, enters=enters, gate=gate, gain=gain, weight=out_weight
    )
    if shares != 2:
        partial = mix(jnp.int32(0), tokens)
        return lax.psum_scatter(partial, "head", scatter_dimension=0, tiled=True).astype(
            jnp.float32
        )
    me = lax.axis_index("head")
    half = tokens // 2
    other = mix((1 - me) * half, half)
    arrived = lax.ppermute(other, "head", [(0, 1), (1, 0)])
    own = mix(me * half, half)
    return own.astype(jnp.float32) + arrived.astype(jnp.float32)


def solution(mesh):
    in_specs = (
        P("ctx", "head", None),
        P("ctx", "head", None),
        P("ctx", "head", None),
        P("ctx", "head", None),
        P("head", "ctx"),
        P("head", "ctx"),
        P(None, "head", None),
        P(None, "head", None),
        P(None, "head", None),
        P(),
        P("head", None),
    )
    out_specs = P(("ctx", "head"), None)
    return jax.shard_map(
        on_device, mesh=mesh, in_specs=in_specs, out_specs=out_specs, check_vma=False
    )
```

```python
import functools

import jax
import jax.numpy as jnp
from jax import lax
from jax.experimental import pallas as pl
from jax.experimental.pallas import tpu as pltpu
from jax.sharding import PartitionSpec as P

norm_epsilon = 1e-06
CHUNK = 128
BASE = 32
RIM = 8
VMEM_LIMIT = 56 * 2**20


def mm(left, right):
    return jnp.dot(
        left.astype(jnp.bfloat16), right.astype(jnp.bfloat16), preferred_element_type=jnp.float32
    )


def silu(value):
    return value / (1.0 + jnp.exp(-value))


def from_behind(value, axis, steps):
    count = lax.axis_size(axis)
    return lax.ppermute(value, axis, [(s, s + steps) for s in range(max(0, count - steps))])


def conv_head(x_ref, rim_ref, w_ref, head, heads, chunk, taps):
    current = x_ref[pl.ds(head, chunk, stride=heads), :]
    padded = jnp.concatenate([rim_ref[pl.ds(head, RIM, stride=heads), :], current], axis=0)
    total = w_ref[(taps - 1) * heads + head : (taps - 1) * heads + head + 1, :] * current
    for back in range(1, taps):
        row = (taps - 1 - back) * heads + head
        total = total + w_ref[row : row + 1, :] * pltpu.roll(padded, back, 0)[RIM:]
    return silu(total)


def unit_rows(matrix, scale=1.0):
    total = jnp.sum(matrix * matrix, axis=-1, keepdims=True)
    return matrix * (lax.rsqrt(total + norm_epsilon) * scale)


def chunk_kernel(
    meta,
    q_ref,
    k_ref,
    v_ref,
    q_rim,
    k_rim,
    v_rim,
    q_w,
    k_w,
    v_w,
    crow_ref,
    brow_ref,
    out_ref,
    fin_ref,
    state,
    q_old,
    k_old,
    v_old,
):
    chunk, kheads, vheads, kfirst, kgroup, taps = meta
    ratio = vheads // kheads
    width = q_ref.shape[1]
    step = pl.program_id(0)

    @pl.when(step == 0)
    def _():
        q_old[...] = q_rim[...]
        k_old[...] = k_rim[...]
        v_old[...] = v_rim[...]
        row = lax.broadcasted_iota(jnp.int32, (width, 2 * width), 0)
        col = lax.broadcasted_iota(jnp.int32, (width, 2 * width), 1)
        start = jnp.where(row == col, 1.0, 0.0)
        for v in range(kgroup * ratio):
            state[v] = start

    row = lax.broadcasted_iota(jnp.int32, (chunk, chunk), 0)
    col = lax.broadcasted_iota(jnp.int32, (chunk, chunk), 1)
    lower = row >= col
    strict = row > col
    eye = jnp.where(row == col, 1.0, 0.0)

    def same(size):
        return (row // size) == (col // size)

    count = kgroup * ratio
    ccol = crow_ref[...].T
    bcol = brow_ref[...].T
    keys_t, lifted, scores, mixing, rhs = [], [], [], [], []
    for i in range(kgroup):
        q = unit_rows(conv_head(q_ref, q_old, q_w, kfirst + i, kheads, chunk, taps), width**-0.5)
        k = unit_rows(conv_head(k_ref, k_old, k_w, kfirst + i, kheads, chunk, taps))
        k_t = k.T.astype(jnp.bfloat16)
        inner = mm(k, k_t)
        cross = mm(q, k_t)
        for r in range(ratio):
            v = i * ratio + r
            values = conv_head(v_ref, v_old, v_w, kfirst * ratio + v, vheads, chunk, taps)
            cc = ccol[:, v : v + 1]
            b = bcol[:, v : v + 1]
            decay = jnp.exp(jnp.minimum(cc - crow_ref[v : v + 1, :], 0.0))
            lift = jnp.exp(cc)
            mixing.append(jnp.where(strict, -(b * inner * decay), 0.0))
            scores.append(jnp.where(lower, cross * decay, 0.0).astype(jnp.bfloat16))
            lifted.append((lift * q).astype(jnp.bfloat16))
            rhs.append(
                jnp.concatenate([b * values, (b * lift) * k], axis=1).astype(jnp.bfloat16)
            )
            keys_t.append(k_t)

    base = min(BASE, chunk)
    near = same(base)
    power = [jnp.where(near, m, 0.0).astype(jnp.bfloat16) for m in mixing]
    inverse = [eye + p.astype(jnp.float32) for p in power]
    power = [mm(p, p).astype(jnp.bfloat16) for p in power]
    reach = 2
    while reach < base:
        if reach * 2 < base:
            both = [
                mm(jnp.concatenate([t.astype(jnp.bfloat16), p], axis=0), p)
                for t, p in zip(inverse, power)
            ]
            inverse = [t + x[:chunk] for t, x in zip(inverse, both)]
            power = [x[chunk:].astype(jnp.bfloat16) for x in both]
        else:
            inverse = [t + mm(t, p) for t, p in zip(inverse, power)]
        reach *= 2
    size = base
    while size < chunk:
        far = same(2 * size) & jnp.logical_not(same(size))
        halves = [t.astype(jnp.bfloat16) for t in inverse]
        links = [mm(jnp.where(far, m, 0.0), t) for m, t in zip(mixing, halves)]
        inverse = [t + mm(h, x) for t, h, x in zip(inverse, halves, links)]
        size *= 2

    solved = [mm(t, r) for t, r in zip(inverse, rhs)]
    states = [state[v] for v in range(count)]
    narrow = [s.astype(jnp.bfloat16) for s in states]
    taken = [mm(x[:, width:], s) for x, s in zip(solved, narrow)]
    update = [
        jnp.concatenate([-w[:, :width], x[:, :width] - w[:, width:]], axis=1)
        for w, x in zip(taken, solved)
    ]
    for v in range(count):
        left = jnp.concatenate([lifted[v], scores[v]], axis=1)
        right = jnp.concatenate([narrow[v], update[v].astype(jnp.bfloat16)], axis=0)
        out_ref[v] = mm(left, right).astype(out_ref.dtype)
        last = crow_ref[v : v + 1, chunk - 1 : chunk]
        fade = jnp.exp(last - ccol[:, v : v + 1])
        state[v] = jnp.exp(last) * states[v] + mm(keys_t[v], fade * update[v])

    for old, ref, heads in ((q_old, q_ref, kheads), (k_old, k_ref, kheads), (v_old, v_ref, vheads)):
        old[...] = ref[(chunk - RIM) * heads : chunk * heads, :]

    @pl.when(step == pl.num_programs(0) - 1)
    def _():
        fin_ref[...] = state[...]


def chunk_call(meta, tokens, width, arrays):
    chunk, kheads, vheads, kfirst, kgroup, taps = meta
    count = kgroup * (vheads // kheads)
    group = kfirst // kgroup

    def whole(rows):
        return pl.BlockSpec((rows, width), lambda c: (0, 0))

    def part(rows):
        return pl.BlockSpec((rows, width), lambda c: (c, 0))

    flops = 2 * tokens * count * width * width * 20
    return pl.pallas_call(
        functools.partial(chunk_kernel, meta),
        grid=(tokens // chunk,),
        in_specs=[
            part(chunk * kheads),
            part(chunk * kheads),
            part(chunk * vheads),
            whole(RIM * kheads),
            whole(RIM * kheads),
            whole(RIM * vheads),
            whole(taps * kheads),
            whole(taps * kheads),
            whole(taps * vheads),
            pl.BlockSpec((count, chunk), lambda c: (group, c)),
            pl.BlockSpec((count, chunk), lambda c: (group, c)),
        ],
        out_specs=[
            pl.BlockSpec((count, chunk, 2 * width), lambda c: (0, c, 0)),
            pl.BlockSpec((count, width, 2 * width), lambda c: (0, 0, 0)),
        ],
        out_shape=[
            jax.ShapeDtypeStruct((count, tokens, 2 * width), jnp.bfloat16),
            jax.ShapeDtypeStruct((count, width, 2 * width), jnp.float32),
        ],
        scratch_shapes=[
            pltpu.VMEM((count, width, 2 * width), jnp.float32),
            pltpu.VMEM((RIM * kheads, width), jnp.float32),
            pltpu.VMEM((RIM * kheads, width), jnp.float32),
            pltpu.VMEM((RIM * vheads, width), jnp.float32),
        ],
        compiler_params=pltpu.CompilerParams(
            dimension_semantics=("arbitrary",), vmem_limit_bytes=VMEM_LIMIT
        ),
        cost_estimate=pl.CostEstimate(
            flops=flops, bytes_accessed=24 * 2**20, transcendentals=tokens * count * width * 4
        ),
    )(*arrays)


def chain_kernel(groups, *refs):
    finals, enter_ref = refs[:groups], refs[groups]
    arrived, leaving, send_sem, recv_sem = refs[groups + 1 :]
    n = lax.axis_size("ctx")
    me = lax.axis_index("ctx")
    right, left = lax.rem(me + 1, n), lax.rem(me + n - 1, n)
    count, width = finals[0].shape[0], finals[0].shape[1]

    barrier = pltpu.get_barrier_semaphore()
    for neighbour in (left, right):
        pl.semaphore_signal(
            barrier, inc=1, device_id={"ctx": neighbour}, device_id_type=pl.DeviceIdType.MESH
        )
    pl.semaphore_wait(barrier, 2)

    def hop(head):
        return pltpu.make_async_remote_copy(
            src_ref=leaving.at[head],
            dst_ref=arrived.at[head],
            send_sem=send_sem.at[head],
            recv_sem=recv_sem.at[head],
            device_id={"ctx": right},
            device_id_type=pl.DeviceIdType.MESH,
        )

    for g in range(groups):
        final = finals[g]

        def turn(v, carry, final=final, g=g):
            head = g * count + v

            through = final[v, :, :width].astype(jnp.bfloat16)
            offset = final[v, :, width:]

            @pl.when(me == 0)
            def _():
                leaving[head] = offset.astype(jnp.bfloat16)
                arrived[head] = jnp.zeros((width, width), jnp.bfloat16)

            @pl.when(me > 0)
            def _():
                hop(head).wait_recv()
                leaving[head] = (mm(through, arrived[head]) + offset).astype(jnp.bfloat16)

            @pl.when(me < n - 1)
            def _():
                hop(head).start()

            enter_ref[head] = arrived[head]
            return carry

        lax.fori_loop(0, count, turn, 0)

    @pl.when(me < n - 1)
    def _():
        def settle(head, carry):
            hop(head).wait_send()
            return carry

        lax.fori_loop(0, groups * count, settle, 0)


def enter_states(finals):
    groups = len(finals)
    count, width, _ = finals[0].shape
    heads = groups * count
    return pl.pallas_call(
        functools.partial(chain_kernel, groups),
        out_shape=jax.ShapeDtypeStruct((heads, width, width), jnp.bfloat16),
        in_specs=[pl.BlockSpec(memory_space=pltpu.VMEM)] * groups,
        out_specs=pl.BlockSpec(memory_space=pltpu.VMEM),
        scratch_shapes=[
            pltpu.VMEM((heads, width, width), jnp.bfloat16),
            pltpu.VMEM((heads, width, width), jnp.bfloat16),
            pltpu.SemaphoreType.DMA((heads,)),
            pltpu.SemaphoreType.DMA((heads,)),
        ],
        compiler_params=pltpu.CompilerParams(
            collective_id=0, has_side_effects=True, vmem_limit_bytes=VMEM_LIMIT
        ),
        cost_estimate=pl.CostEstimate(
            flops=2 * heads * width**3, bytes_accessed=12 * heads * width**2, transcendentals=0
        ),
    )(*finals)


def mix_kernel(groups, rows, vheads, first_ref, *refs):
    outs = refs[:groups]
    enter_ref, gate_ref, gain_ref, weight_ref, part_ref, normed = refs[groups:]
    width = gain_ref.shape[1]
    count = vheads // groups
    for g in range(groups):
        for v in range(count):
            head = g * count + v
            own = outs[g][v]
            recurrent = own[:, width:].astype(jnp.float32) + mm(own[:, :width], enter_ref[head])
            mean = jnp.sum(recurrent * recurrent, axis=-1, keepdims=True) * (1.0 / width)
            gate = gate_ref[pl.ds(head, rows, stride=vheads), :]
            scaled = recurrent * lax.rsqrt(mean + norm_epsilon) * gain_ref[...] * silu(gate)
            normed[:, head * width : (head + 1) * width] = scaled.astype(jnp.bfloat16)
    depth, columns = weight_ref.shape
    piece = min(512, columns)
    for c in range(0, columns, piece):
        part_ref[:, c : c + piece] = jnp.dot(
            normed[...], weight_ref[:, c : c + piece], preferred_element_type=jnp.float32
        ).astype(jnp.bfloat16)


def mix_call(first, tokens, outs, enters, gate, gain, weight):
    groups = len(outs)
    count, all_tokens, double = outs[0].shape
    width = double // 2
    vheads = gate.shape[0] // all_tokens
    rows = min(256, tokens)
    depth, columns = weight.shape
    spec = pltpu.PrefetchScalarGridSpec(
        num_scalar_prefetch=1,
        grid=(tokens // rows,),
        in_specs=[pl.BlockSpec((count, rows, double), lambda t, s: (0, s[0] + t, 0))] * groups
        + [
            pl.BlockSpec((vheads, width, width), lambda t, s: (0, 0, 0)),
            pl.BlockSpec((rows * vheads, width), lambda t, s: (s[0] + t, 0)),
            pl.BlockSpec((1, width), lambda t, s: (0, 0)),
            pl.BlockSpec((depth, columns), lambda t, s: (0, 0)),
        ],
        out_specs=pl.BlockSpec((rows, columns), lambda t, s: (t, 0)),
        scratch_shapes=[pltpu.VMEM((rows, depth), jnp.bfloat16)],
    )
    return pl.pallas_call(
        functools.partial(mix_kernel, groups, rows, vheads),
        grid_spec=spec,
        out_shape=jax.ShapeDtypeStruct((tokens, columns), jnp.bfloat16),
        compiler_params=pltpu.CompilerParams(
            dimension_semantics=("arbitrary",), vmem_limit_bytes=VMEM_LIMIT
        ),
        cost_estimate=pl.CostEstimate(
            flops=2 * tokens * depth * columns,
            bytes_accessed=2 * depth * columns + 16 * tokens * depth,
            transcendentals=tokens * depth,
        ),
    )((first // rows).astype(jnp.int32).reshape(1), *outs, enters, gate, gain, weight)


def on_device(
    query_in,
    key_in,
    value_in,
    gate_in,
    log_gate,
    strength,
    query_conv,
    key_conv,
    value_conv,
    norm_gain,
    out_weight,
):
    tokens, kheads, width = query_in.shape
    vheads = value_in.shape[1]
    taps = query_conv.shape[0]
    ratio = vheads // kheads
    chunk = min(CHUNK, tokens)
    rim = taps - 1

    def flat(array):
        return array.reshape(-1, width)

    rims = from_behind(
        jnp.concatenate([a[-rim:] for a in (query_in, key_in, value_in)], axis=1), "ctx", 1
    )
    rims = jnp.pad(rims, ((RIM - rim, 0), (0, 0), (0, 0)))
    q_rim, k_rim, v_rim = (
        flat(rims[:, a:b])
        for a, b in ((0, kheads), (kheads, 2 * kheads), (2 * kheads, 2 * kheads + vheads))
    )
    upper = jnp.triu(jnp.ones((chunk, chunk), jnp.float32))
    summed = jnp.einsum(
        "hnm,mc->hnc",
        log_gate.reshape(vheads, tokens // chunk, chunk),
        upper,
        precision=lax.Precision.HIGHEST,
    ).reshape(vheads, tokens)

    kgroup = min(4, kheads)
    outs, finals = [], []
    for kfirst in range(0, kheads, kgroup):
        out, final = chunk_call(
            (chunk, kheads, vheads, kfirst, kgroup, taps),
            tokens,
            width,
            (
                flat(query_in),
                flat(key_in),
                flat(value_in),
                q_rim,
                k_rim,
                v_rim,
                flat(query_conv),
                flat(key_conv),
                flat(value_conv),
                summed,
                strength,
            ),
        )
        outs.append(out)
        finals.append(final)
    enters = enter_states(finals)

    shares = lax.axis_size("head")
    gate = flat(gate_in)
    gain = norm_gain.reshape(1, width)
    mix = functools.partial(
        mix_call, outs=outs, enters=enters, gate=gate, gain=gain, weight=out_weight
    )
    if shares != 2:
        partial = mix(jnp.int32(0), tokens)
        return lax.psum_scatter(partial, "head", scatter_dimension=0, tiled=True).astype(
            jnp.float32
        )
    me = lax.axis_index("head")
    half = tokens // 2
    other = mix((1 - me) * half, half)
    arrived = lax.ppermute(other, "head", [(0, 1), (1, 0)])
    own = mix(me * half, half)
    return own.astype(jnp.float32) + arrived.astype(jnp.float32)


def solution(mesh):
    in_specs = (
        P("ctx", "head", None),
        P("ctx", "head", None),
        P("ctx", "head", None),
        P("ctx", "head", None),
        P("head", "ctx"),
        P("head", "ctx"),
        P(None, "head", None),
        P(None, "head", None),
        P(None, "head", None),
        P(),
        P("head", None),
    )
    out_specs = P(("ctx", "head"), None)
    return jax.shard_map(
        on_device, mesh=mesh, in_specs=in_specs, out_specs=out_specs, check_vma=False
    )
```
